512 devices in a mesh: stream: 4 (over y), frame: 32 (over z, core), head: 4 (over x).
Axes of the slice: x: 4, y: 4, z: 16, core: 2. Of those that a mesh axis runs over, the one named last changes fastest.
Arguments:
- queries: bfloat16 [32768, 3072], P(('stream', 'frame'), 'head'), parts along dimension 0, may hold values from -8 to 8
- keys: bfloat16 [32768, 512], P(('stream', 'frame'), 'head'), parts along dimension 0, may hold values from -8 to 8
- values: bfloat16 [32768, 512], P(('stream', 'frame'), 'head'), parts along dimension 0, may hold values from -6 to 6
- block_mask: int32 [256, 64], P('stream'), parts along dimension 0, may hold values from 0 to 1, as said below
- section_ids: int32 [256], P('stream'), parts along dimension 0, may hold values from 0 to 3
- section_gate: float32 [4, 3072], P(None, 'head'), may hold values from 0.25 to 12
- norm_gain: float32 [3072], P('head'), may hold values from 0.1 to 1.9
Outputs:
- branch_out: bfloat16 [32768, 3072], P(('stream', 'frame'), 'head'), parts along dimension 0
The draws below stay inside these ranges and needn't reach their ends.
There are 4 independent parts, one for each index of `stream`. The reference program is written for one: setup_inputs(seed, part) draws one part's arguments, and reference() takes and returns one part's arrays. A program takes and returns all parts, laid end to end along the dimension named above; an argument that names none is the same for every part. Nothing has to cross between parts.
Inputs may be any that keep to these rules, and one draw needn't show every extreme that they name: `block_mask`: row c is 1 on a run of spans that ends at span c, and 0 elsewhere.
All inputs are finite; a program needn't handle non-finite values.
Results may differ from the reference program's by a relative error of at most 0.017.
Values may be sent and summed in bfloat16 or wider, within the bound.
No kernel may reach another device: no remote copies, remote signals or barrier semaphores. Data moves between devices by JAX's collectives and lax.ppermute only.
A program may use at most 64 MiB of HBM per device.

```python
import jax
import jax.numpy as jnp
from jax import lax

HEADS = 24
KV_HEADS = 4
HEAD_DIM = 128
BLOCK = 128
SECTIONS = 4
BLOCKS = 64
TOKENS = 8192
Q_WIDTH = 3072
KV_WIDTH = 512


def draw_queries(key, part):
    key = jax.random.fold_in(key, 11)
    return jnp.clip(jax.random.normal(key, (TOKENS, HEADS * HEAD_DIM), jnp.float32), -6.0, 6.0).astype(jnp.bfloat16)


def draw_keys(key, part):
    key = jax.random.fold_in(key, 13)
    return jnp.clip(jax.random.normal(key, (TOKENS, KV_HEADS * HEAD_DIM), jnp.float32), -6.0, 6.0).astype(jnp.bfloat16)


def draw_block_mask(key, part):
    key = jax.random.fold_in(key, 5)
    row_index = jnp.arange(BLOCKS, dtype=jnp.int32)
    raw_draw = jax.random.randint(key, (BLOCKS,), 0, 1 << 20)
    least_reach = row_index // 4
    reach_back = least_reach + raw_draw % (row_index - least_reach + 1)
    col_index = row_index[None, :]
    inside = (col_index <= row_index[:, None]) & (col_index >= row_index[:, None] - reach_back[:, None])
    return inside.astype(jnp.int32)


def draw_section_gate(key, part):
    key = jax.random.fold_in(key, 7)
    column_share = jnp.arange(HEADS * HEAD_DIM, dtype=jnp.float32) / (HEADS * HEAD_DIM - 1)
    base_gate = jnp.exp(jax.random.uniform(key, (SECTIONS, HEADS * HEAD_DIM), jnp.float32, jnp.log(0.25), jnp.log(4.0)))
    rise_factor = 3.0 ** (0.5 * column_share)
    return base_gate * rise_factor[None, :]


def place_ends(array, rng, low, high):
    place = [jax.random.randint(jax.random.fold_in(rng, axis), (), 0, length) for axis, length in enumerate(array.shape)]
    widest = array.shape.index(max(array.shape))
    next_to = place[:widest] + [(place[widest] + 1) % array.shape[widest]] + place[widest + 1:]
    return array.at[tuple(place)].set(low).at[tuple(next_to)].set(high)


def steps_of(key, dims, shards, low, high):
    factor_of = 1.0
    for position, parts in shards:
        steps = jax.random.uniform(jax.random.fold_in(jax.random.fold_in(key, 6), position), (parts,), jnp.float32, low / len(shards), high / len(shards))
        factor_of = factor_of * jnp.repeat(jnp.exp(steps), dims[position] // parts).reshape((-1,) + (1,) * (len(dims) - 1 - position))
    return factor_of


def bell_draw(rng, dims, scale, most, shards=(), kind=jnp.bfloat16):
    level = steps_of(rng, dims, shards, -0.22, 0.18) if shards else 1.0
    result = jax.random.normal(rng, dims, jnp.float32) * scale * level
    return jnp.minimum(jnp.maximum(result, -most), most).astype(kind)


def setup_inputs(seed: int = 0, part: int = 0) -> dict:
    arg_keys = jax.random.split(jax.random.key(seed), 8)
    part_keys = jax.random.split(jax.random.fold_in(arg_keys[7], part), 8)
    queries = draw_queries(jax.random.fold_in(jax.random.fold_in(arg_keys[7], part), 71), part)
    keys = draw_keys(jax.random.fold_in(jax.random.fold_in(arg_keys[7], part), 71), part)
    values = bell_draw(part_keys[2], (TOKENS, KV_WIDTH), 1.0, 6.0, ((0, 32), (1, 4)))
    block_mask = draw_block_mask(jax.random.fold_in(jax.random.fold_in(arg_keys[7], part), 71), part)
    section_ids = place_ends(jax.random.randint(part_keys[4], (BLOCKS,), 0, SECTIONS), jax.random.fold_in(part_keys[4], 1), 0, SECTIONS - 1).astype(jnp.int32)
    section_gate = draw_section_gate(jax.random.fold_in(arg_keys[7], 71), part)
    norm_gain = jnp.clip(1.0 + 0.18 * jax.random.normal(arg_keys[6], (Q_WIDTH,), jnp.float32), 0.1, 1.9)
    return {"queries": queries, "keys": keys, "values": values, "block_mask": block_mask, "section_ids": section_ids, "section_gate": section_gate, "norm_gain": norm_gain}


def block_places():
    numbers = jnp.arange(BLOCKS, dtype=jnp.int32)
    owners = numbers // 2
    return jnp.where(numbers % 2 == 0, owners, BLOCKS - 1 - owners)

def reference(queries, keys, values, block_mask, section_ids, section_gate, norm_gain):
    group_size = HEADS // KV_HEADS
    softmax_scale = HEAD_DIM ** (-0.5)
    places = block_places()
    key_places = jnp.repeat(places, BLOCK)
    keys_wide = keys.astype(jnp.float32).reshape(TOKENS, KV_HEADS, HEAD_DIM)
    values_wide = values.astype(jnp.float32).reshape(TOKENS, KV_HEADS, HEAD_DIM)

    def one_block(block_number):
        query_block = lax.dynamic_slice_in_dim(queries, block_number * BLOCK, BLOCK, 0)
        query_block = query_block.astype(jnp.float32).reshape(BLOCK, KV_HEADS, group_size, HEAD_DIM)
        query_place = places[block_number]
        live_keys = block_mask[query_place][key_places] != 0
        scores = jnp.einsum('cgrd,kgd->cgrk', query_block, keys_wide) * softmax_scale
        scores = jnp.where(live_keys, scores, -jnp.inf)
        row_max = lax.optimization_barrier(jnp.max(scores, axis=-1, keepdims=True))
        weights = jnp.exp(scores - row_max)
        row_total = lax.optimization_barrier(jnp.sum(weights, axis=-1))
        rounded = lax.optimization_barrier(weights.astype(jnp.bfloat16)).astype(jnp.float32)
        attended = jnp.einsum('cgrk,kgd->cgrd', rounded, values_wide) / row_total[..., None]
        gated = attended.reshape(BLOCK, Q_WIDTH) * section_gate[section_ids[query_place]][None, :]
        mean_square = lax.optimization_barrier(jnp.mean(gated * gated, axis=1, keepdims=True))
        return (gated * lax.rsqrt(mean_square + 1e-06) * norm_gain[None, :]).astype(jnp.bfloat16)
    result_blocks = lax.map(one_block, jnp.arange(BLOCKS, dtype=jnp.int32))
    return result_blocks.reshape(TOKENS, Q_WIDTH)
```

```python
import functools
import math

import jax
import jax.numpy as jnp
from jax import lax
from jax.experimental import pallas as pl
from jax.experimental.pallas import tpu as pltpu
from jax.sharding import PartitionSpec as P

HEADS = 24
HEAD_DIM = 128
LOCAL_HEADS = 6
BLOCK = 128
BLOCKS = 64
CHIPS = 16
EPS = 1e-06
TO_LOG2 = HEAD_DIM ** (-0.5) * math.log2(math.e)
LOW = -1e30
VMEM_BYTES = 24 * 1024 * 1024


def attend_body(pieces, first, last, *refs):
    refs = list(refs)
    meta, q_ref = refs.pop(0), refs.pop(0)
    pieces_in = [refs.pop(0) for _ in pieces]
    if not first:
        state_in = [refs.pop(0) for _ in range(3)]
    if last:
        ids_ref, gate_ref = refs.pop(0), refs.pop(0)
        gated_ref, square_ref = refs.pop(0), refs.pop(0)
        acc_ref, sum_ref, max_ref = refs.pop(0), refs.pop(0), refs.pop(0)
    else:
        acc_ref, sum_ref, max_ref = refs.pop(0), refs.pop(0), refs.pop(0)
    buf, table, sems = refs

    copies = []
    tile = 0
    frame = meta[2, 0]
    chip = frame // 2
    core = frame % 2
    for number, ((how, distance), ref) in enumerate(zip(pieces, pieces_in)):
        tiles = ref.shape[0] // 256
        copy = pltpu.make_async_copy(ref, buf.at[pl.ds(tile * 256, tiles * 256)], sems.at[number])
        copy.start()
        copies.append(copy)
        sign = {"own": 0, "mine": -1, "theirs": 1}[how.split("_")[0]]
        source = lax.rem(chip + sign * (1 - 2 * core) * distance + CHIPS, CHIPS)
        if how == "mine_half":
            table[tile, 0], table[tile, 1] = source, core
        elif how == "theirs_half":
            table[tile, 0], table[tile, 1] = source, 1 - core
        else:
            for part in range(2):
                table[tile + part, 0], table[tile + part, 1] = source, jnp.int32(part)
        tile += tiles
    if first:
        acc_ref[...] = jnp.zeros_like(acc_ref)
        sum_ref[...] = jnp.zeros_like(sum_ref)
        max_ref[...] = jnp.full_like(max_ref, LOW)
    else:
        outs = (acc_ref, sum_ref, max_ref)
        for number, (src, dst) in enumerate(zip(state_in, outs)):
            copy = pltpu.make_async_copy(src, dst, sems.at[len(pieces) + number])
            copy.start()
            copies.append(copy)
    for copy in copies:
        copy.wait()

    lane = lax.broadcasted_iota(jnp.int32, (1, 256), 1)
    ones = jnp.ones((256, HEAD_DIM), jnp.bfloat16)

    def step(index, carry):
        slot = index % 2
        number = index // 2
        source, part = table[number, 0], table[number, 1]
        place_a = jnp.where(part == 0, 2 * source, BLOCKS - 1 - 2 * source)
        place_b = jnp.where(part == 0, 2 * source + 1, BLOCKS - 2 - 2 * source)
        live_a, live_b = meta[slot, place_a], meta[slot, place_b]

        @pl.when(live_a + live_b > 0)
        def _():
            rows = pl.ds(pl.multiple_of(slot * BLOCK, BLOCK), BLOCK)
            keys_at = pl.ds(pl.multiple_of(number * 256, 256), 256)
            key_tile = buf[keys_at, :HEAD_DIM]
            value_tile = jnp.concatenate([buf[keys_at, HEAD_DIM:], ones], axis=1)
            low_a = jnp.where(live_a > 0, 0.0, LOW).astype(jnp.float32)
            low_b = jnp.where(live_b > 0, 0.0, LOW).astype(jnp.float32)
            bias = jnp.where(lane < BLOCK, low_a, low_b)
            for head in range(LOCAL_HEADS):
                cols = slice(head * HEAD_DIM, (head + 1) * HEAD_DIM)
                scores = lax.dot_general(
                    q_ref[rows, cols], key_tile, (((1,), (1,)), ((), ())),
                    preferred_element_type=jnp.float32,
                )
                scores = scores * TO_LOG2 + bias
                prior = max_ref[rows, cols]
                now = jnp.maximum(prior, jnp.max(scores, axis=1, keepdims=True))
                weights = jnp.exp2(scores - jnp.concatenate([now, now], axis=1))
                shrink = jnp.exp2(prior - now)
                added = jnp.dot(
                    weights.astype(jnp.bfloat16), value_tile, preferred_element_type=jnp.float32
                )
                acc_ref[rows, cols] = acc_ref[rows, cols] * shrink + added[:, :HEAD_DIM]
                sum_ref[rows, cols] = sum_ref[rows, cols] * shrink + added[:, HEAD_DIM:]
                max_ref[rows, cols] = now

        return carry

    lax.fori_loop(0, 2 * tile, step, 0)

    if last:
        places = (frame, BLOCKS - 1 - frame)
        eye = lax.broadcasted_iota(jnp.int32, (BLOCK, BLOCK), 0) == lax.broadcasted_iota(
            jnp.int32, (BLOCK, BLOCK), 1
        )
        for slot in range(2):
            rows = slice(slot * BLOCK, (slot + 1) * BLOCK)
            gate_row = gate_ref[pl.ds(ids_ref[places[slot]], 1), :]
            total = jnp.zeros((BLOCK, HEAD_DIM), jnp.float32)
            for head in range(LOCAL_HEADS):
                cols = slice(head * HEAD_DIM, (head + 1) * HEAD_DIM)
                gated = acc_ref[rows, cols] / sum_ref[rows, cols] * gate_row[:, cols]
                gated_ref[rows, cols] = gated
                total = total + gated * gated
            row_total = jnp.sum(total, axis=1, keepdims=True)
            square_ref[slot : slot + 1, :] = jnp.sum(
                jnp.where(eye, row_total, 0.0), axis=0, keepdims=True
            )


def attend(pieces, arrays, meta, queries, state, finish=None):
    first, last = state is None, finish is not None
    tiles = sum(array.shape[0] // 256 for array in arrays)
    rows, cols = queries.shape
    wide = jax.ShapeDtypeStruct((rows, cols), jnp.float32)
    vmem, smem, anywhere = (
        pl.BlockSpec(memory_space=pltpu.VMEM),
        pl.BlockSpec(memory_space=pltpu.SMEM),
        pl.BlockSpec(memory_space=pl.ANY),
    )
    operands = [meta, queries, *arrays]
    in_specs = [smem, vmem] + [anywhere] * len(arrays)
    scratch = [
        pltpu.VMEM((tiles * 256, 256), jnp.bfloat16),
        pltpu.SMEM((max(tiles, 2), 2), jnp.int32),
        pltpu.SemaphoreType.DMA((len(arrays) + 3,)),
    ]
    if not first:
        operands += list(state)
        in_specs += [anywhere] * 3
    if last:
        operands += list(finish)
        in_specs += [smem, vmem]
        out_shape = [wide, jax.ShapeDtypeStruct((2, BLOCK), jnp.float32)]
        scratch = [pltpu.VMEM((rows, cols), jnp.float32)] * 3 + scratch
    else:
        out_shape = [wide] * 3
    pairs = tiles * 2 * LOCAL_HEADS
    return pl.pallas_call(
        functools.partial(attend_body, pieces, first, last),
        out_shape=out_shape,
        in_specs=in_specs,
        out_specs=[vmem] * len(out_shape),
        scratch_shapes=scratch,
        compiler_params=pltpu.CompilerParams(vmem_limit_bytes=VMEM_BYTES),
        cost_estimate=pl.CostEstimate(
            flops=pairs * 4 * BLOCK * 256 * HEAD_DIM,
            bytes_accessed=8 * rows * cols * 4,
            transcendentals=pairs * BLOCK * 256,
        ),
    )(*operands)


def gather_pair_body(core_ref, own_ref, other_ref, out_ref):
    core = core_ref[2, 0] % 2
    for half in range(2):
        at = 256 * half
        out_ref[pl.ds(pl.multiple_of(at + 128 * core, 128), 128), :] = own_ref[half * 128 : half * 128 + 128, :]
        out_ref[pl.ds(pl.multiple_of(at + 128 * (1 - core), 128), 128), :] = other_ref[half * 128 : half * 128 + 128, :]


def gather_pair(meta, own, other):
    return pl.pallas_call(
        gather_pair_body,
        out_shape=jax.ShapeDtypeStruct((512, 256), jnp.bfloat16),
        in_specs=[pl.BlockSpec(memory_space=pltpu.SMEM)] + [pl.BlockSpec(memory_space=pltpu.VMEM)] * 2,
        out_specs=pl.BlockSpec(memory_space=pltpu.VMEM),
        compiler_params=pltpu.CompilerParams(vmem_limit_bytes=VMEM_BYTES),
    )(meta, own, other)


def scale_body(gated_ref, square_ref, gain_ref, out_ref):
    eye = lax.broadcasted_iota(jnp.int32, (BLOCK, BLOCK), 0) == lax.broadcasted_iota(
        jnp.int32, (BLOCK, BLOCK), 1
    )
    for slot in range(2):
        rows = slice(slot * BLOCK, (slot + 1) * BLOCK)
        scale = lax.rsqrt(square_ref[slot : slot + 1, :] / (HEADS * HEAD_DIM) + EPS)
        column = jnp.sum(jnp.where(eye, scale, 0.0), axis=1, keepdims=True)
        out_ref[rows, :] = (gated_ref[rows, :] * column * gain_ref[...]).astype(jnp.bfloat16)


def scale_rows(gated, squares, gain):
    return pl.pallas_call(
        scale_body,
        out_shape=jax.ShapeDtypeStruct(gated.shape, jnp.bfloat16),
        in_specs=[pl.BlockSpec(memory_space=pltpu.VMEM)] * 3,
        out_specs=pl.BlockSpec(memory_space=pltpu.VMEM),
        compiler_params=pltpu.CompilerParams(vmem_limit_bytes=VMEM_BYTES),
    )(gated, squares, gain)


def along(hops):
    return [(2 * z, 2 * ((z + hops) % CHIPS)) for z in range(CHIPS)] + [
        (2 * z + 1, 2 * ((z - hops) % CHIPS) + 1) for z in range(CHIPS)
    ]


def send(array, hops):
    return lax.ppermute(array, "frame", along(hops))


def swap(array):
    return lax.ppermute(array, "frame", [(d, d ^ 1) for d in range(2 * CHIPS)])


def body(queries, keys, values, block_mask, section_ids, section_gate, norm_gain):
    frame = lax.axis_index("frame")
    own = jnp.concatenate([keys, values], axis=1)
    meta = jnp.concatenate(
        [
            lax.dynamic_slice_in_dim(block_mask, frame, 1, 0),
            lax.dynamic_slice_in_dim(block_mask, BLOCKS - 1 - frame, 1, 0),
            jnp.full((1, BLOCKS), frame, jnp.int32),
        ],
        axis=0,
    )
    core = frame % 2
    chunk = gather_pair(meta, own, swap(own))

    s3 = send(chunk, 3)
    s1 = send(chunk, 1)
    s2 = send(chunk, 2)
    state = attend([("own", 0)], [chunk], meta, queries, None)

    s6 = send(s3, 3)
    s4 = send(s3, 1)
    s5 = send(s3, 2)
    w123 = swap(jnp.concatenate([s1, s2, s3], axis=0))
    state = attend([("mine", 1), ("mine", 2), ("mine", 3)], [s1, s2, s3], meta, queries, state)
    w123 = [w123[512 * i : 512 * i + 512] for i in range(3)]
    state = attend([("theirs", 1), ("theirs", 2), ("theirs", 3)], w123, meta, queries, state)

    s7 = send(s6, 1)
    half = lax.dynamic_slice_in_dim(s6, 256 * core, 256, 0)
    s8 = send(half, 2)
    w456 = swap(jnp.concatenate([s4, s5, s6], axis=0))
    state = attend([("mine", 4), ("mine", 5), ("mine", 6)], [s4, s5, s6], meta, queries, state)
    w456 = [w456[512 * i : 512 * i + 512] for i in range(3)]
    state = attend([("theirs", 4), ("theirs", 5), ("theirs", 6)], w456, meta, queries, state)

    w78 = swap(jnp.concatenate([s7, s8], axis=0))
    state = attend([("mine", 7), ("mine_half", 8)], [s7, s8], meta, queries, state)
    gated, squares = attend(
        [("theirs", 7), ("theirs_half", 8)],
        [w78[:512], w78[512:]],
        meta,
        queries,
        state,
        (section_ids, section_gate),
    )
    squares = lax.psum(squares, "head")
    return scale_rows(gated, squares, norm_gain.reshape(1, -1))


def solution(mesh):
    in_specs = (
        P(("stream", "frame"), "head"),
        P(("stream", "frame"), "head"),
        P(("stream", "frame"), "head"),
        P("stream", None),
        P("stream"),
        P(None, "head"),
        P("head"),
    )
    out_specs = P(("stream", "frame"), "head")
    return jax.shard_map(body, mesh=mesh, in_specs=in_specs, out_specs=out_specs, check_vma=False)
```

```python
import functools
import math

import jax
import jax.numpy as jnp
from jax import lax
from jax.experimental import pallas as pl
from jax.experimental.pallas import tpu as pltpu
from jax.sharding import PartitionSpec as P

HEADS = 24
HEAD_DIM = 128
LOCAL_HEADS = 6
BLOCK = 128
BLOCKS = 64
CHIPS = 16
EPS = 1e-06
TO_LOG2 = HEAD_DIM ** (-0.5) * math.log2(math.e)
LOW = -1e30
VMEM_BYTES = 16 * 1024 * 1024


def attend_body(pieces, first, emit, last, *refs):
    refs = list(refs)
    meta, q_ref = refs.pop(0), refs.pop(0)
    pieces_in = [refs.pop(0) for _ in pieces]
    if not first:
        del refs[:3]
    acc_ref, sum_ref, max_ref = refs.pop(0), refs.pop(0), refs.pop(0)
    if last:
        pack_ref = refs.pop(0)
    if emit:
        buf = refs.pop(0)
        table, sems = refs
    elif last:
        buf, table, sems, level_rows = refs
    else:
        buf, table, sems = refs

    frame = meta[4, 0]
    chip = frame // 2
    core = frame % 2
    copies = []
    places = []
    for number, (chunks, ref) in enumerate(zip(pieces, pieces_in)):
        to = buf.at[pl.ds(len(places) * 256, ref.shape[0])]
        copies.append(pltpu.make_async_copy(ref, to, sems.at[number]))
        for how, distance in chunks:
            source = lax.rem(chip - (1 - 2 * core) * distance + CHIPS, CHIPS)
            low = (2 * source, 2 * source + 1)
            high = (BLOCKS - 1 - 2 * source, BLOCKS - 2 - 2 * source)
            if how == "own":
                places.append((frame, BLOCKS - 1 - frame))
            elif how == "whole":
                places += [low, high]
            else:
                places.append(tuple(jnp.where(core == 0, one, other) for one, other in zip(low, high)))

    for copy in copies:
        copy.start()

    counts = []
    for slot in range(4):
        count = jnp.int32(0)
        for number, (place_a, place_b) in enumerate(places):
            live_a, live_b = meta[slot, place_a], meta[slot, place_b]
            at = 4 * count + slot
            table[at, 0], table[at, 1], table[at, 2] = jnp.int32(number), live_a, live_b
            count = count + jnp.where(live_a + live_b > 0, 1, 0)
        counts.append(count)
        for extra in range(2):
            at = 4 * (count + extra) + slot
            table[at, 0], table[at, 1], table[at, 2] = jnp.int32(0), jnp.int32(0), jnp.int32(0)
    if first:
        acc_ref[...] = jnp.zeros_like(acc_ref)
        sum_ref[...] = jnp.zeros_like(sum_ref)
        max_ref[...] = jnp.full_like(max_ref, LOW)
    for copy in copies:
        copy.wait()

    span = lax.broadcasted_iota(jnp.int32, (1, 256), 1) < BLOCK
    abreast = min(sum(len(chunks) for chunks in pieces), len(places))
    ones = jnp.ones((256 * abreast, HEAD_DIM), jnp.bfloat16)

    def low_if_dead(live):
        return jnp.where(live > 0, 0.0, LOW).astype(jnp.float32)

    def per_slot(slot, carry):
        rows = pl.ds(pl.multiple_of(slot * BLOCK, BLOCK), BLOCK)
        heads = [slice(head * HEAD_DIM, (head + 1) * HEAD_DIM) for head in range(LOCAL_HEADS)]
        count = jnp.where(
            slot < 2,
            jnp.where(slot == 0, counts[0], counts[1]),
            jnp.where(slot == 2, counts[2], counts[3]),
        )

        def per_tiles(index, carry):
            keys_in, values_in, bias_in = [], [], []
            for tile in range(abreast):
                at = 4 * (abreast * index + tile) + slot
                tile_rows = pl.ds(pl.multiple_of(table[at, 0] * 256, 256), 256)
                keys_in.append(buf[tile_rows, :HEAD_DIM])
                values_in.append(buf[tile_rows, HEAD_DIM:])
                bias_in.append(jnp.where(span, low_if_dead(table[at, 1]), low_if_dead(table[at, 2])))
            keys = jnp.concatenate(keys_in, axis=0)
            values = jnp.concatenate([jnp.concatenate(values_in, axis=0), ones], axis=1)
            bias = jnp.concatenate(bias_in, axis=1)
            before = [(max_ref[rows, cols], acc_ref[rows, cols], sum_ref[rows, cols]) for cols in heads]
            scores_of = [
                lax.dot_general(
                    q_ref[rows, cols], keys, (((1,), (1,)), ((), ())), preferred_element_type=jnp.float32
                )
                for cols in heads
            ]
            results = []
            for scores, (prior, acc, total) in zip(scores_of, before):
                scores = scores + bias
                now = jnp.maximum(prior, jnp.max(scores, axis=1, keepdims=True))
                top = now * TO_LOG2
                weights = jnp.exp2(scores * TO_LOG2 - jnp.concatenate([top] * (2 * abreast), axis=1))
                shrink = jnp.exp2(prior * TO_LOG2 - top)
                added = jnp.dot(
                    weights.astype(jnp.bfloat16), values, preferred_element_type=jnp.float32
                )
                results.append(
                    (now, acc * shrink + added[:, :HEAD_DIM], total * shrink + added[:, HEAD_DIM:])
                )
            for cols, (now, acc, total) in zip(heads, results):
                max_ref[rows, cols], acc_ref[rows, cols], sum_ref[rows, cols] = now, acc, total
            return carry

        lax.fori_loop(0, (count + abreast - 1) // abreast, per_tiles, 0)
        return carry

    lax.fori_loop(0, 4, per_slot, 0)

    if last:
        eye = diagonal()
        for slot in range(2):
            rows = slice((2 + slot) * BLOCK, (3 + slot) * BLOCK)
            to = slice(slot * BLOCK, (slot + 1) * BLOCK)
            for head in range(LOCAL_HEADS):
                cols = slice(head * HEAD_DIM, (head + 1) * HEAD_DIM)
                total = jnp.maximum(sum_ref[rows, cols], 1e-30)
                pack_ref[to, cols] = (acc_ref[rows, cols] / total).astype(jnp.bfloat16)
                level = max_ref[rows, cols] * TO_LOG2 + jnp.log2(total)
                level = jnp.sum(jnp.where(eye, level, 0.0), axis=0, keepdims=True)
                parts = []
                for _ in range(3):
                    part = level.astype(jnp.bfloat16).astype(jnp.float32)
                    level = level - part
                    parts.append(part)
                parts.append(jnp.zeros((5, HEAD_DIM), jnp.float32))
                level_rows[8 * slot : 8 * slot + 8, cols] = jnp.concatenate(parts, axis=0)
        pack_ref[2 * BLOCK :, :] = level_rows[...].astype(jnp.bfloat16)


def diagonal():
    return lax.broadcasted_iota(jnp.int32, (BLOCK, BLOCK), 0) == lax.broadcasted_iota(
        jnp.int32, (BLOCK, BLOCK), 1
    )


def attend(pieces, arrays, meta, queries, state, emit=False, last=False):
    first = state is None
    tiles = sum(array.shape[0] // 256 for array in arrays)
    rows, cols = queries.shape
    wide = jax.ShapeDtypeStruct((rows, cols), jnp.float32)
    vmem, smem, anywhere = (
        pl.BlockSpec(memory_space=pltpu.VMEM),
        pl.BlockSpec(memory_space=pltpu.SMEM),
        pl.BlockSpec(memory_space=pl.ANY),
    )
    operands = [meta, queries, *arrays]
    in_specs = [smem, vmem] + [anywhere] * len(arrays)
    scratch = [
        pltpu.VMEM((tiles * 256, 256), jnp.bfloat16),
        pltpu.SMEM((4 * tiles + 16, 4), jnp.int32),
        pltpu.SemaphoreType.DMA((len(arrays),)),
    ]
    aliases = {}
    if not first:
        aliases = {len(operands) + number: number for number in range(3)}
        operands += list(state)
        in_specs += [vmem] * 3
    out_shape = [wide] * 3
    if emit:
        out_shape.append(jax.ShapeDtypeStruct((tiles * 256, 256), jnp.bfloat16))
        scratch = scratch[1:]
    if last:
        out_shape.append(jax.ShapeDtypeStruct((rows // 2 + 16, cols), jnp.bfloat16))
        scratch.append(pltpu.VMEM((16, cols), jnp.float32))
    pairs = tiles * 4 * LOCAL_HEADS
    return pl.pallas_call(
        functools.partial(attend_body, pieces, first, emit, last),
        out_shape=out_shape,
        in_specs=in_specs,
        out_specs=[vmem] * len(out_shape),
        scratch_shapes=scratch,
        input_output_aliases=aliases,
        compiler_params=pltpu.CompilerParams(vmem_limit_bytes=VMEM_BYTES),
        cost_estimate=pl.CostEstimate(
            flops=pairs * 4 * BLOCK * 256 * HEAD_DIM,
            bytes_accessed=8 * rows * cols * 4,
            transcendentals=pairs * BLOCK * 256,
        ),
    )(*operands)


def finish_body(frame_ref, ids_ref, gate_ref, acc_ref, sum_ref, max_ref, theirs, gated_ref, square_ref):
    frame = frame_ref[4, 0]
    places = (frame, BLOCKS - 1 - frame)
    eye = diagonal()
    for slot in range(2):
        rows = slice(slot * BLOCK, (slot + 1) * BLOCK)
        gate_row = gate_ref[pl.ds(ids_ref[places[slot]], 1), :]
        parts = theirs[2 * BLOCK + 8 * slot : 2 * BLOCK + 8 * slot + 8, :].astype(jnp.float32)
        levels = parts[0:1] + parts[1:2] + parts[2:3]
        total = jnp.zeros((BLOCK, HEAD_DIM), jnp.float32)
        for head in range(LOCAL_HEADS):
            cols = slice(head * HEAD_DIM, (head + 1) * HEAD_DIM)
            level = jnp.sum(jnp.where(eye, levels[:, cols], 0.0), axis=1, keepdims=True)
            prior = max_ref[rows, cols] * TO_LOG2
            top = jnp.maximum(prior, level)
            mine, yours = jnp.exp2(prior - top), jnp.exp2(level - top)
            joined = acc_ref[rows, cols] * mine + theirs[rows, cols].astype(jnp.float32) * yours
            gated = joined / (sum_ref[rows, cols] * mine + yours) * gate_row[:, cols]
            gated_ref[rows, cols] = gated
            total = total + gated * gated
        row_total = jnp.sum(total, axis=1, keepdims=True)
        square_ref[slot : slot + 1, :] = jnp.sum(jnp.where(eye, row_total, 0.0), axis=0, keepdims=True)


def finish(meta, section_ids, section_gate, state, theirs):
    cols = theirs.shape[1]
    vmem, smem = pl.BlockSpec(memory_space=pltpu.VMEM), pl.BlockSpec(memory_space=pltpu.SMEM)
    return pl.pallas_call(
        finish_body,
        out_shape=[
            jax.ShapeDtypeStruct((2 * BLOCK, cols), jnp.float32),
            jax.ShapeDtypeStruct((2, BLOCK), jnp.float32),
        ],
        in_specs=[smem, smem] + [vmem] * 5,
        out_specs=[vmem, vmem],
        compiler_params=pltpu.CompilerParams(vmem_limit_bytes=VMEM_BYTES),
    )(meta, section_ids, section_gate, *state, theirs)


def pack_body(keys_ref, values_ref, queries_ref, out_ref, sems):
    copies = []
    at = 0
    for number, ref in enumerate((keys_ref, values_ref, queries_ref)):
        to = out_ref.at[:, at : at + ref.shape[1]]
        copies.append(pltpu.make_async_copy(ref, to, sems.at[number]))
        at += ref.shape[1]
    for copy in copies:
        copy.start()
    for copy in copies:
        copy.wait()


def pack(keys, values, queries):
    anywhere = pl.BlockSpec(memory_space=pltpu.HBM)
    cols = keys.shape[1] + values.shape[1] + queries.shape[1]
    return pl.pallas_call(
        pack_body,
        out_shape=jax.ShapeDtypeStruct((keys.shape[0], cols), keys.dtype),
        in_specs=[anywhere] * 3,
        out_specs=pl.BlockSpec(memory_space=pltpu.VMEM),
        scratch_shapes=[pltpu.SemaphoreType.DMA((3,))],
        compiler_params=pltpu.CompilerParams(vmem_limit_bytes=VMEM_BYTES),
    )(keys, values, queries)


def gather_pair_body(frame_ref, own_ref, other_ref, chunk_ref, both_ref, mine_ref, sems):
    core = frame_ref[0] % 2
    copies = [
        pltpu.make_async_copy(own_ref.at[:, 256:], both_ref.at[0:256], sems.at[0]),
        pltpu.make_async_copy(other_ref.at[:, 256:], both_ref.at[256:512], sems.at[1]),
        pltpu.make_async_copy(own_ref.at[:, :256], mine_ref, sems.at[2]),
    ]
    for half in range(2):
        rows = slice(half * BLOCK, (half + 1) * BLOCK)
        for number, (ref, place) in enumerate(((own_ref, core), (other_ref, 1 - core))):
            to = chunk_ref.at[pl.ds(pl.multiple_of(256 * half + BLOCK * place, BLOCK), BLOCK)]
            copies.append(
                pltpu.make_async_copy(ref.at[rows, :256], to, sems.at[3 + 2 * half + number])
            )
    for copy in copies:
        copy.start()
    for copy in copies:
        copy.wait()


def gather_pair(frame, own, other):
    rows, cols = own.shape
    vmem = pl.BlockSpec(memory_space=pltpu.VMEM)
    return pl.pallas_call(
        gather_pair_body,
        out_shape=[
            jax.ShapeDtypeStruct((2 * rows, 256), own.dtype),
            jax.ShapeDtypeStruct((2 * rows, cols - 256), own.dtype),
            jax.ShapeDtypeStruct((rows, 256), own.dtype),
        ],
        in_specs=[pl.BlockSpec(memory_space=pltpu.SMEM), vmem, vmem],
        out_specs=[vmem] * 3,
        scratch_shapes=[pltpu.SemaphoreType.DMA((7,))],
        compiler_params=pltpu.CompilerParams(vmem_limit_bytes=VMEM_BYTES),
    )(frame, own, other)


def half_body(which, frame_ref, chunk_ref, out_ref, sem):
    rows = out_ref.shape[0]
    part = frame_ref[0] % 2 if which is None else jnp.int32(which)
    at = pl.multiple_of(rows * part, rows)
    copy = pltpu.make_async_copy(chunk_ref.at[pl.ds(at, rows)], out_ref, sem)
    copy.start()
    copy.wait()


def half_of(frame, array, which=None):
    rows, cols = array.shape
    vmem = pl.BlockSpec(memory_space=pltpu.VMEM)
    return pl.pallas_call(
        functools.partial(half_body, which),
        out_shape=jax.ShapeDtypeStruct((rows // 2, cols), array.dtype),
        in_specs=[pl.BlockSpec(memory_space=pltpu.SMEM), vmem],
        out_specs=vmem,
        scratch_shapes=[pltpu.SemaphoreType.DMA],
        compiler_params=pltpu.CompilerParams(vmem_limit_bytes=VMEM_BYTES),
    )(frame, array)


def scale_body(gated_ref, square_ref, gain_ref, out_ref):
    eye = lax.broadcasted_iota(jnp.int32, (BLOCK, BLOCK), 0) == lax.broadcasted_iota(
        jnp.int32, (BLOCK, BLOCK), 1
    )
    for slot in range(2):
        rows = slice(slot * BLOCK, (slot + 1) * BLOCK)
        scale = lax.rsqrt(square_ref[slot : slot + 1, :] / (HEADS * HEAD_DIM) + EPS)
        column = jnp.sum(jnp.where(eye, scale, 0.0), axis=1, keepdims=True)
        out_ref[rows, :] = (gated_ref[rows, :] * column * gain_ref[...]).astype(jnp.bfloat16)


def scale_rows(gated, squares, gain):
    return pl.pallas_call(
        scale_body,
        out_shape=jax.ShapeDtypeStruct(gated.shape, jnp.bfloat16),
        in_specs=[pl.BlockSpec(memory_space=pltpu.VMEM)] * 3,
        out_specs=pl.BlockSpec(memory_space=pltpu.VMEM),
        compiler_params=pltpu.CompilerParams(vmem_limit_bytes=VMEM_BYTES),
    )(gated, squares, gain)


def along(hops):
    return [(2 * z, 2 * ((z + hops) % CHIPS)) for z in range(CHIPS)] + [
        (2 * z + 1, 2 * ((z - hops) % CHIPS) + 1) for z in range(CHIPS)
    ]


def send(array, hops):
    return lax.ppermute(array, "frame", along(hops))


def swap(array):
    return lax.ppermute(array, "frame", [(d, d ^ 1) for d in range(2 * CHIPS)])


def after(array, state):
    array, *state = lax.optimization_barrier((array, *state))
    return array, state


def body(queries, keys, values, block_mask, section_ids, section_gate, norm_gain):
    frame = lax.axis_index("frame")
    here = frame.reshape(1)
    own = pack(keys, values, queries)
    chunk, both, mine = gather_pair(here, own, swap(own))
    places = [frame, BLOCKS - 1 - frame, frame ^ 1, BLOCKS - 1 - (frame ^ 1)]
    meta = jnp.concatenate(
        [lax.dynamic_slice_in_dim(block_mask, place, 1, 0) for place in places]
        + [jnp.full((1, BLOCKS), frame, jnp.int32)],
        axis=0,
    )
    s3 = send(chunk, 3)
    s1 = send(chunk, 1)
    state = attend([[("own", 0)]], [mine], meta, both, None)
    s3, state = after(s3, state)
    s6 = send(s3, 3)
    s4 = send(s3, 1)
    s2 = send(s1, 1)
    state = attend([[("whole", 1)], [("whole", 3)]], [s1, s3], meta, both, state)
    s6, state = after(s6, state)
    s7 = send(s6, 1)
    s8 = send(half_of(here, s6), 2)
    s5 = send(s4, 1)
    state = attend([[("whole", 2)], [("whole", 4)], [("whole", 6)]], [s2, s4, s6], meta, both, state)
    *state, theirs = attend(
        [[("whole", 5)], [("whole", 7)], [("half", 8)]], [s5, s7, s8], meta, both, state, last=True
    )
    gated, squares = finish(meta, section_ids, section_gate, state, swap(theirs))
    squares = lax.psum(squares, "head")
    return scale_rows(gated, squares, norm_gain.reshape(1, -1))


def solution(mesh):
    in_specs = (
        P(("stream", "frame"), "head"),
        P(("stream", "frame"), "head"),
        P(("stream", "frame"), "head"),
        P("stream", None),
        P("stream"),
        P(None, "head"),
        P("head"),
    )
    out_specs = P(("stream", "frame"), "head")
    return jax.shard_map(body, mesh=mesh, in_specs=in_specs, out_specs=out_specs, check_vma=False)
```

```python
import functools
import math

import jax
import jax.numpy as jnp
from jax import lax
from jax.experimental import pallas as pl
from jax.experimental.pallas import tpu as pltpu
from jax.sharding import PartitionSpec as P

HEADS = 24
HEAD_DIM = 128
LOCAL_HEADS = 6
BLOCK = 128
BLOCKS = 64
CHIPS = 16
EPS = 1e-06
TO_LOG2 = HEAD_DIM ** (-0.5) * math.log2(math.e)
LOW = -1e30
VMEM_BYTES = 16 * 1024 * 1024


def attend_body(pieces, first, last, *refs):
    refs = list(refs)
    meta, q_ref = refs.pop(0), refs.pop(0)
    arrays = [refs.pop(0) for _ in pieces]
    if not first:
        del refs[:3]
    acc_ref, sum_ref, max_ref = refs.pop(0), refs.pop(0), refs.pop(0)
    if last:
        pack_ref, level_rows = refs

    frame = meta[4, 0]
    chip = frame // 2
    core = frame % 2
    groups = [[], []]
    for ref, (how, distance) in zip(arrays, pieces):
        source = lax.rem(chip - (1 - 2 * core) * distance + CHIPS, CHIPS)
        low = (2 * source, 2 * source + 1)
        high = (BLOCKS - 1 - 2 * source, BLOCKS - 2 - 2 * source)
        if how == "own":
            groups[0].append((ref, slice(0, 256), (frame, BLOCKS - 1 - frame)))
        elif how == "whole":
            groups[0].append((ref, slice(0, 256), low))
            groups[1].append((ref, slice(256, 512), high))
        else:
            places = tuple(jnp.where(core == 0, one, other) for one, other in zip(low, high))
            groups[0].append((ref, slice(0, 256), places))
    if first:
        acc_ref[...] = jnp.zeros_like(acc_ref)
        sum_ref[...] = jnp.zeros_like(sum_ref)
        max_ref[...] = jnp.full_like(max_ref, LOW)
    heads = [slice(head * HEAD_DIM, (head + 1) * HEAD_DIM) for head in range(LOCAL_HEADS)]

    def add(tiles, slot, lives):
        rows = pl.ds(pl.multiple_of(slot * BLOCK, BLOCK), BLOCK)
        width = 256 * len(tiles)
        keys = jnp.concatenate([ref[at, :HEAD_DIM] for ref, at, _ in tiles], axis=0)
        values = jnp.concatenate([ref[at, HEAD_DIM:] for ref, at, _ in tiles], axis=0)
        values = jnp.concatenate([values, jnp.ones((width, HEAD_DIM), jnp.bfloat16)], axis=1)
        before = [(max_ref[rows, cols], acc_ref[rows, cols], sum_ref[rows, cols]) for cols in heads]
        scores_of = [
            lax.dot_general(
                q_ref[rows, cols], keys, (((1,), (1,)), ((), ())), preferred_element_type=jnp.float32
            )
            for cols in heads
        ]
        if lives is not None:
            bias = jnp.concatenate(
                [
                    jnp.broadcast_to(jnp.where(live > 0, 0.0, LOW).astype(jnp.float32), (1, BLOCK))
                    for live in lives
                ],
                axis=1,
            )
            scores_of = [scores + bias for scores in scores_of]
        results = []
        for scores, (prior, acc, total) in zip(scores_of, before):
            now = jnp.maximum(prior, jnp.max(scores, axis=1, keepdims=True))
            top = now * TO_LOG2
            weights = jnp.exp2(scores * TO_LOG2 - jnp.concatenate([top] * (width // BLOCK), axis=1))
            shrink = jnp.exp2(prior * TO_LOG2 - top)
            added = jnp.dot(weights.astype(jnp.bfloat16), values, preferred_element_type=jnp.float32)
            results.append((now, acc * shrink + added[:, :HEAD_DIM], total * shrink + added[:, HEAD_DIM:]))
        for cols, (now, acc, total) in zip(heads, results):
            max_ref[rows, cols], acc_ref[rows, cols], sum_ref[rows, cols] = now, acc, total

    for tiles in groups:
        if not tiles:
            continue

        def per_slot(slot, carry, tiles=tiles):
            lives = [meta[slot, place] for _, _, places in tiles for place in places]
            count = sum(lives)

            @pl.when(count == len(lives))
            def _():
                add(tiles, slot, None)

            @pl.when(jnp.logical_and(count > 0, count < len(lives)))
            def _():
                add(tiles, slot, lives)

            return carry

        lax.fori_loop(0, 4, per_slot, 0)

    if last:
        eye = diagonal()
        for slot in range(2):
            rows = slice((2 + slot) * BLOCK, (3 + slot) * BLOCK)
            to = slice(slot * BLOCK, (slot + 1) * BLOCK)
            for head in range(LOCAL_HEADS):
                cols = slice(head * HEAD_DIM, (head + 1) * HEAD_DIM)
                total = jnp.maximum(sum_ref[rows, cols], 1e-30)
                pack_ref[to, cols] = (acc_ref[rows, cols] / total).astype(jnp.bfloat16)
                level = max_ref[rows, cols] * TO_LOG2 + jnp.log2(total)
                level = jnp.sum(jnp.where(eye, level, 0.0), axis=0, keepdims=True)
                parts = []
                for _ in range(3):
                    part = level.astype(jnp.bfloat16).astype(jnp.float32)
                    level = level - part
                    parts.append(part)
                parts.append(jnp.zeros((5, HEAD_DIM), jnp.float32))
                level_rows[8 * slot : 8 * slot + 8, cols] = jnp.concatenate(parts, axis=0)
        pack_ref[2 * BLOCK :, :] = level_rows[...].astype(jnp.bfloat16)


def diagonal():
    return lax.broadcasted_iota(jnp.int32, (BLOCK, BLOCK), 0) == lax.broadcasted_iota(
        jnp.int32, (BLOCK, BLOCK), 1
    )


def attend(pieces, arrays, meta, queries, state, last=False):
    first = state is None
    tiles = sum(array.shape[0] // 256 for array in arrays)
    rows, cols = queries.shape
    vmem, smem = pl.BlockSpec(memory_space=pltpu.VMEM), pl.BlockSpec(memory_space=pltpu.SMEM)
    operands = [meta, queries, *arrays]
    in_specs = [smem] + [vmem] * (1 + len(arrays))
    aliases = {}
    if not first:
        aliases = {len(operands) + number: number for number in range(3)}
        operands += list(state)
        in_specs += [vmem] * 3
    out_shape = [jax.ShapeDtypeStruct((rows, cols), jnp.float32)] * 3
    scratch = []
    if last:
        out_shape.append(jax.ShapeDtypeStruct((rows // 2 + 16, cols), jnp.bfloat16))
        scratch.append(pltpu.VMEM((16, cols), jnp.float32))
    pairs = tiles * 4 * LOCAL_HEADS
    return pl.pallas_call(
        functools.partial(attend_body, pieces, first, last),
        out_shape=out_shape,
        in_specs=in_specs,
        out_specs=[vmem] * len(out_shape),
        scratch_shapes=scratch,
        input_output_aliases=aliases,
        compiler_params=pltpu.CompilerParams(vmem_limit_bytes=VMEM_BYTES),
        cost_estimate=pl.CostEstimate(
            flops=pairs * 4 * BLOCK * 256 * HEAD_DIM,
            bytes_accessed=8 * rows * cols * 4,
            transcendentals=pairs * BLOCK * 256,
        ),
    )(*operands)


def finish_body(frame_ref, ids_ref, gate_ref, acc_ref, sum_ref, max_ref, theirs, gated_ref, square_ref):
    frame = frame_ref[4, 0]
    places = (frame, BLOCKS - 1 - frame)
    eye = diagonal()
    for slot in range(2):
        rows = slice(slot * BLOCK, (slot + 1) * BLOCK)
        gate_row = gate_ref[pl.ds(ids_ref[places[slot]], 1), :]
        parts = theirs[2 * BLOCK + 8 * slot : 2 * BLOCK + 8 * slot + 8, :].astype(jnp.float32)
        levels = parts[0:1] + parts[1:2] + parts[2:3]
        total = jnp.zeros((BLOCK, HEAD_DIM), jnp.float32)
        for head in range(LOCAL_HEADS):
            cols = slice(head * HEAD_DIM, (head + 1) * HEAD_DIM)
            level = jnp.sum(jnp.where(eye, levels[:, cols], 0.0), axis=1, keepdims=True)
            prior = max_ref[rows, cols] * TO_LOG2
            top = jnp.maximum(prior, level)
            mine, yours = jnp.exp2(prior - top), jnp.exp2(level - top)
            joined = acc_ref[rows, cols] * mine + theirs[rows, cols].astype(jnp.float32) * yours
            gated = joined / (sum_ref[rows, cols] * mine + yours) * gate_row[:, cols]
            gated_ref[rows, cols] = gated
            total = total + gated * gated
        row_total = jnp.sum(total, axis=1, keepdims=True)
        square_ref[slot : slot + 1, :] = jnp.sum(jnp.where(eye, row_total, 0.0), axis=0, keepdims=True)


def finish(meta, section_ids, section_gate, state, theirs):
    cols = theirs.shape[1]
    vmem, smem = pl.BlockSpec(memory_space=pltpu.VMEM), pl.BlockSpec(memory_space=pltpu.SMEM)
    return pl.pallas_call(
        finish_body,
        out_shape=[
            jax.ShapeDtypeStruct((2 * BLOCK, cols), jnp.float32),
            jax.ShapeDtypeStruct((2, BLOCK), jnp.float32),
        ],
        in_specs=[smem, smem] + [vmem] * 5,
        out_specs=[vmem, vmem],
        compiler_params=pltpu.CompilerParams(vmem_limit_bytes=VMEM_BYTES),
    )(meta, section_ids, section_gate, *state, theirs)


def pack_body(keys_ref, values_ref, queries_ref, out_ref, sems):
    copies = []
    at = 0
    for number, ref in enumerate((keys_ref, values_ref, queries_ref)):
        to = out_ref.at[:, at : at + ref.shape[1]]
        copies.append(pltpu.make_async_copy(ref, to, sems.at[number]))
        at += ref.shape[1]
    for copy in copies:
        copy.start()
    for copy in copies:
        copy.wait()


def pack(keys, values, queries):
    anywhere = pl.BlockSpec(memory_space=pltpu.HBM)
    cols = keys.shape[1] + values.shape[1] + queries.shape[1]
    return pl.pallas_call(
        pack_body,
        out_shape=jax.ShapeDtypeStruct((keys.shape[0], cols), keys.dtype),
        in_specs=[anywhere] * 3,
        out_specs=pl.BlockSpec(memory_space=pltpu.VMEM),
        scratch_shapes=[pltpu.SemaphoreType.DMA((3,))],
        compiler_params=pltpu.CompilerParams(vmem_limit_bytes=VMEM_BYTES),
    )(*(pltpu.with_memory_space_constraint(array, pltpu.HBM) for array in (keys, values, queries)))


def gather_pair_body(frame_ref, own_ref, other_ref, chunk_ref, both_ref, mine_ref, sems):
    core = frame_ref[0] % 2
    copies = [
        pltpu.make_async_copy(own_ref.at[:, 256:], both_ref.at[0:256], sems.at[0]),
        pltpu.make_async_copy(other_ref.at[:, 256:], both_ref.at[256:512], sems.at[1]),
        pltpu.make_async_copy(own_ref.at[:, :256], mine_ref, sems.at[2]),
    ]
    for half in range(2):
        rows = slice(half * BLOCK, (half + 1) * BLOCK)
        for number, (ref, place) in enumerate(((own_ref, core), (other_ref, 1 - core))):
            to = chunk_ref.at[pl.ds(pl.multiple_of(256 * half + BLOCK * place, BLOCK), BLOCK)]
            copies.append(
                pltpu.make_async_copy(ref.at[rows, :256], to, sems.at[3 + 2 * half + number])
            )
    for copy in copies:
        copy.start()
    for copy in copies:
        copy.wait()


def gather_pair(frame, own, other):
    rows, cols = own.shape
    vmem = pl.BlockSpec(memory_space=pltpu.VMEM)
    return pl.pallas_call(
        gather_pair_body,
        out_shape=[
            jax.ShapeDtypeStruct((2 * rows, 256), own.dtype),
            jax.ShapeDtypeStruct((2 * rows, cols - 256), own.dtype),
            jax.ShapeDtypeStruct((rows, 256), own.dtype),
        ],
        in_specs=[pl.BlockSpec(memory_space=pltpu.SMEM), vmem, vmem],
        out_specs=[vmem] * 3,
        scratch_shapes=[pltpu.SemaphoreType.DMA((7,))],
        compiler_params=pltpu.CompilerParams(vmem_limit_bytes=VMEM_BYTES),
    )(frame, own, other)


def half_body(which, frame_ref, chunk_ref, out_ref, sem):
    rows = out_ref.shape[0]
    part = frame_ref[0] % 2 if which is None else jnp.int32(which)
    at = pl.multiple_of(rows * part, rows)
    copy = pltpu.make_async_copy(chunk_ref.at[pl.ds(at, rows)], out_ref, sem)
    copy.start()
    copy.wait()


def half_of(frame, array, which=None):
    rows, cols = array.shape
    vmem = pl.BlockSpec(memory_space=pltpu.VMEM)
    return pl.pallas_call(
        functools.partial(half_body, which),
        out_shape=jax.ShapeDtypeStruct((rows // 2, cols), array.dtype),
        in_specs=[pl.BlockSpec(memory_space=pltpu.SMEM), vmem],
        out_specs=vmem,
        scratch_shapes=[pltpu.SemaphoreType.DMA],
        compiler_params=pltpu.CompilerParams(vmem_limit_bytes=VMEM_BYTES),
    )(frame, array)


def scale_body(gated_ref, square_ref, gain_ref, out_ref):
    eye = lax.broadcasted_iota(jnp.int32, (BLOCK, BLOCK), 0) == lax.broadcasted_iota(
        jnp.int32, (BLOCK, BLOCK), 1
    )
    for slot in range(2):
        rows = slice(slot * BLOCK, (slot + 1) * BLOCK)
        square = sum(square_ref[part, slot : slot + 1, :] for part in range(square_ref.shape[0]))
        scale = lax.rsqrt(square / (HEADS * HEAD_DIM) + EPS)
        column = jnp.sum(jnp.where(eye, scale, 0.0), axis=1, keepdims=True)
        out_ref[rows, :] = (gated_ref[rows, :] * column * gain_ref[...]).astype(jnp.bfloat16)


def scale_rows(gated, squares, gain):
    return pl.pallas_call(
        scale_body,
        out_shape=jax.ShapeDtypeStruct(gated.shape, jnp.bfloat16),
        in_specs=[pl.BlockSpec(memory_space=pltpu.VMEM)] * 3,
        out_specs=pl.BlockSpec(memory_space=pltpu.VMEM),
        compiler_params=pltpu.CompilerParams(vmem_limit_bytes=VMEM_BYTES),
    )(gated, squares, gain)


def along(hops):
    return [(2 * z, 2 * ((z + hops) % CHIPS)) for z in range(CHIPS)] + [
        (2 * z + 1, 2 * ((z - hops) % CHIPS) + 1) for z in range(CHIPS)
    ]


def send(array, hops):
    return lax.ppermute(array, "frame", along(hops))


def swap(array):
    return lax.ppermute(array, "frame", [(d, d ^ 1) for d in range(2 * CHIPS)])


def after(array, state):
    array, *state = lax.optimization_barrier((array, *state))
    return array, state


def body(queries, keys, values, block_mask, section_ids, section_gate, norm_gain):
    frame = lax.axis_index("frame")
    here = frame.reshape(1)
    own = pack(keys, values, queries)
    chunk, both, mine = gather_pair(here, own, swap(own))
    places = [frame, BLOCKS - 1 - frame, frame ^ 1, BLOCKS - 1 - (frame ^ 1)]
    meta = jnp.concatenate(
        [lax.dynamic_slice_in_dim(block_mask, place, 1, 0) for place in places]
        + [jnp.full((1, BLOCKS), frame, jnp.int32)],
        axis=0,
    )
    s3 = send(chunk, 3)
    s1 = send(chunk, 1)
    state = attend([("own", 0)], [mine], meta, both, None)
    s3, state = after(s3, state)
    s6 = send(s3, 3)
    s4 = send(s3, 1)
    s2 = send(s1, 1)
    state = attend([("whole", 1), ("whole", 3)], [s1, s3], meta, both, state)
    s6, state = after(s6, state)
    s7 = send(s6, 1)
    s8 = send(half_of(here, s6), 2)
    s5 = send(s4, 1)
    state = attend([("whole", 2), ("whole", 4), ("whole", 6)], [s2, s4, s6], meta, both, state)
    *state, theirs = attend(
        [("whole", 5), ("whole", 7), ("half", 8)], [s5, s7, s8], meta, both, state, last=True
    )
    gated, squares = finish(meta, section_ids, section_gate, state, swap(theirs))
    squares = lax.all_gather(squares, "head", axis=0)
    return scale_rows(gated, squares, norm_gain.reshape(1, -1))


def solution(mesh):
    in_specs = (
        P(("stream", "frame"), "head"),
        P(("stream", "frame"), "head"),
        P(("stream", "frame"), "head"),
        P("stream", None),
        P("stream"),
        P(None, "head"),
        P("head"),
    )
    out_specs = P(("stream", "frame"), "head")
    return jax.shard_map(body, mesh=mesh, in_specs=in_specs, out_specs=out_specs, check_vma=False)
```

```python
import functools
import math

import jax
import jax.numpy as jnp
from jax import lax
from jax.experimental import pallas as pl
from jax.experimental.pallas import tpu as pltpu
from jax.sharding import PartitionSpec as P

HEADS = 24
HEAD_DIM = 128
LOCAL_HEADS = 6
BLOCK = 128
BLOCKS = 64
CHIPS = 16
EPS = 1e-06
TO_LOG2 = HEAD_DIM ** (-0.5) * math.log2(math.e)
LOW = -1e30
VMEM_BYTES = 16 * 1024 * 1024


def attend_body(pieces, first, last, *refs):
    refs = list(refs)
    meta, q_ref = refs.pop(0), refs.pop(0)
    arrays = [refs.pop(0) for _ in pieces]
    if not first:
        del refs[:3]
    acc_ref, sum_ref, max_ref = refs.pop(0), refs.pop(0), refs.pop(0)
    if last:
        pack_ref, level_rows = refs

    frame = meta[4, 0]
    chip = frame // 2
    core = frame % 2
    groups = [[], []]
    for ref, (how, distance) in zip(arrays, pieces):
        source = lax.rem(chip - (1 - 2 * core) * distance + CHIPS, CHIPS)
        low = (2 * source, 2 * source + 1)
        high = (BLOCKS - 1 - 2 * source, BLOCKS - 2 - 2 * source)
        if how == "own":
            groups[0].append((ref, slice(0, 256), (frame, BLOCKS - 1 - frame)))
        elif how == "whole":
            groups[0].append((ref, slice(0, 256), low))
            groups[1].append((ref, slice(256, 512), high))
        else:
            places = tuple(jnp.where(core == 0, one, other) for one, other in zip(low, high))
            groups[0].append((ref, slice(0, 256), places))
    if first:
        acc_ref[...] = jnp.zeros_like(acc_ref)
        sum_ref[...] = jnp.zeros_like(sum_ref)
        max_ref[...] = jnp.full_like(max_ref, LOW)
    heads = [slice(head * HEAD_DIM, (head + 1) * HEAD_DIM) for head in range(LOCAL_HEADS)]

    def add(tiles, slot, lives):
        rows = pl.ds(pl.multiple_of(slot * BLOCK, BLOCK), BLOCK)
        width = 256 * len(tiles)
        keys = jnp.concatenate([ref[at, :HEAD_DIM] for ref, at, _ in tiles], axis=0)
        values = jnp.concatenate([ref[at, HEAD_DIM:] for ref, at, _ in tiles], axis=0)
        values = jnp.concatenate([values, jnp.ones((width, HEAD_DIM), jnp.bfloat16)], axis=1)
        before = [(max_ref[rows, cols], acc_ref[rows, cols], sum_ref[rows, cols]) for cols in heads]
        scores_of = [
            lax.dot_general(
                q_ref[rows, cols], keys, (((1,), (1,)), ((), ())), preferred_element_type=jnp.float32
            )
            for cols in heads
        ]
        if lives is not None:
            bias = jnp.concatenate(
                [
                    jnp.broadcast_to(jnp.where(live > 0, 0.0, LOW).astype(jnp.float32), (1, BLOCK))
                    for live in lives
                ],
                axis=1,
            )
            scores_of = [scores + bias for scores in scores_of]
        results = []
        for scores, (prior, acc, total) in zip(scores_of, before):
            now = jnp.maximum(prior, jnp.max(scores, axis=1, keepdims=True))
            top = now * TO_LOG2
            weights = jnp.exp2(scores * TO_LOG2 - jnp.concatenate([top] * (width // BLOCK), axis=1))
            shrink = jnp.exp2(prior * TO_LOG2 - top)
            added = jnp.dot(weights.astype(jnp.bfloat16), values, preferred_element_type=jnp.float32)
            results.append((now, acc * shrink + added[:, :HEAD_DIM], total * shrink + added[:, HEAD_DIM:]))
        for cols, (now, acc, total) in zip(heads, results):
            max_ref[rows, cols], acc_ref[rows, cols], sum_ref[rows, cols] = now, acc, total

    for tiles in groups:
        if not tiles:
            continue

        def per_slot(slot, carry, tiles=tiles):
            lives = [meta[slot, place] for _, _, places in tiles for place in places]
            count = sum(lives)

            @pl.when(count == len(lives))
            def _():
                add(tiles, slot, None)

            @pl.when(jnp.logical_and(count > 0, count < len(lives)))
            def _():
                add(tiles, slot, lives)

            return carry

        lax.fori_loop(0, 4, per_slot, 0)

    if last:
        eye = diagonal()
        for slot in range(2):
            rows = slice((2 + slot) * BLOCK, (3 + slot) * BLOCK)
            to = slice(slot * BLOCK, (slot + 1) * BLOCK)
            for head in range(LOCAL_HEADS):
                cols = slice(head * HEAD_DIM, (head + 1) * HEAD_DIM)
                total = jnp.maximum(sum_ref[rows, cols], 1e-30)
                pack_ref[to, cols] = (acc_ref[rows, cols] / total).astype(jnp.bfloat16)
                level = max_ref[rows, cols] * TO_LOG2 + jnp.log2(total)
                level = jnp.sum(jnp.where(eye, level, 0.0), axis=0, keepdims=True)
                parts = []
                for _ in range(3):
                    part = level.astype(jnp.bfloat16).astype(jnp.float32)
                    level = level - part
                    parts.append(part)
                parts.append(jnp.zeros((5, HEAD_DIM), jnp.float32))
                level_rows[8 * slot : 8 * slot + 8, cols] = jnp.concatenate(parts, axis=0)
        pack_ref[2 * BLOCK :, :] = level_rows[...].astype(jnp.bfloat16)


def diagonal():
    return lax.broadcasted_iota(jnp.int32, (BLOCK, BLOCK), 0) == lax.broadcasted_iota(
        jnp.int32, (BLOCK, BLOCK), 1
    )


def attend(pieces, arrays, meta, queries, state, last=False):
    first = state is None
    tiles = sum(array.shape[0] // 256 for array in arrays)
    rows, cols = queries.shape
    vmem, smem = pl.BlockSpec(memory_space=pltpu.VMEM), pl.BlockSpec(memory_space=pltpu.SMEM)
    operands = [meta, queries, *arrays]
    in_specs = [smem] + [vmem] * (1 + len(arrays))
    aliases = {}
    if not first:
        aliases = {len(operands) + number: number for number in range(3)}
        operands += list(state)
        in_specs += [vmem] * 3
    out_shape = [jax.ShapeDtypeStruct((rows, cols), jnp.float32)] * 3
    scratch = []
    if last:
        out_shape.append(jax.ShapeDtypeStruct((rows // 2 + 16, cols), jnp.bfloat16))
        scratch.append(pltpu.VMEM((16, cols), jnp.float32))
    pairs = tiles * 4 * LOCAL_HEADS
    return pl.pallas_call(
        functools.partial(attend_body, pieces, first, last),
        out_shape=out_shape,
        in_specs=in_specs,
        out_specs=[vmem] * len(out_shape),
        scratch_shapes=scratch,
        input_output_aliases=aliases,
        compiler_params=pltpu.CompilerParams(vmem_limit_bytes=VMEM_BYTES),
        cost_estimate=pl.CostEstimate(
            flops=pairs * 4 * BLOCK * 256 * HEAD_DIM,
            bytes_accessed=8 * rows * cols * 4,
            transcendentals=pairs * BLOCK * 256,
        ),
    )(*operands)


def finish_body(frame_ref, ids_ref, gate_ref, acc_ref, sum_ref, max_ref, theirs, gated_ref, square_ref):
    frame = frame_ref[4, 0]
    places = (frame, BLOCKS - 1 - frame)
    eye = diagonal()
    for slot in range(2):
        rows = slice(slot * BLOCK, (slot + 1) * BLOCK)
        gate_row = gate_ref[pl.ds(ids_ref[places[slot]], 1), :]
        parts = theirs[2 * BLOCK :, :].astype(jnp.float32)[8 * slot : 8 * slot + 3]
        levels = parts[0:1] + parts[1:2] + parts[2:3]
        total = jnp.zeros((BLOCK, HEAD_DIM), jnp.float32)
        for head in range(LOCAL_HEADS):
            cols = slice(head * HEAD_DIM, (head + 1) * HEAD_DIM)
            level = jnp.sum(jnp.where(eye, levels[:, cols], 0.0), axis=1, keepdims=True)
            prior = max_ref[rows, cols] * TO_LOG2
            top = jnp.maximum(prior, level)
            mine, yours = jnp.exp2(prior - top), jnp.exp2(level - top)
            joined = acc_ref[rows, cols] * mine + theirs[rows, cols].astype(jnp.float32) * yours
            gated = joined / (sum_ref[rows, cols] * mine + yours) * gate_row[:, cols]
            gated_ref[rows, cols] = gated
            total = total + gated * gated
        row_total = jnp.sum(total, axis=1, keepdims=True)
        square_ref[slot : slot + 1, :] = jnp.sum(jnp.where(eye, row_total, 0.0), axis=0, keepdims=True)


def finish(meta, section_ids, section_gate, state, theirs):
    cols = theirs.shape[1]
    vmem, smem = pl.BlockSpec(memory_space=pltpu.VMEM), pl.BlockSpec(memory_space=pltpu.SMEM)
    return pl.pallas_call(
        finish_body,
        out_shape=[
            jax.ShapeDtypeStruct((2 * BLOCK, cols), jnp.float32),
            jax.ShapeDtypeStruct((2, BLOCK), jnp.float32),
        ],
        in_specs=[smem, smem] + [vmem] * 5,
        out_specs=[vmem, vmem],
        compiler_params=pltpu.CompilerParams(vmem_limit_bytes=VMEM_BYTES),
    )(meta, section_ids, section_gate, *state, theirs)


def pack_body(keys_ref, values_ref, queries_ref, out_ref, sems):
    copies = []
    at = 0
    for number, ref in enumerate((keys_ref, values_ref, queries_ref)):
        to = out_ref.at[:, at : at + ref.shape[1]]
        copies.append(pltpu.make_async_copy(ref, to, sems.at[number]))
        at += ref.shape[1]
    for copy in copies:
        copy.start()
    for copy in copies:
        copy.wait()


def pack(keys, values, queries):
    anywhere = pl.BlockSpec(memory_space=pltpu.HBM)
    cols = keys.shape[1] + values.shape[1] + queries.shape[1]
    return pl.pallas_call(
        pack_body,
        out_shape=jax.ShapeDtypeStruct((keys.shape[0], cols), keys.dtype),
        in_specs=[anywhere] * 3,
        out_specs=pl.BlockSpec(memory_space=pltpu.VMEM),
        scratch_shapes=[pltpu.SemaphoreType.DMA((3,))],
        compiler_params=pltpu.CompilerParams(vmem_limit_bytes=VMEM_BYTES),
    )(*(pltpu.with_memory_space_constraint(array, pltpu.HBM) for array in (keys, values, queries)))


def gather_pair_body(frame_ref, own_ref, other_ref, chunk_ref, both_ref, mine_ref, sems):
    core = frame_ref[0] % 2
    copies = [
        pltpu.make_async_copy(own_ref.at[:, 256:], both_ref.at[0:256], sems.at[0]),
        pltpu.make_async_copy(other_ref.at[:, 256:], both_ref.at[256:512], sems.at[1]),
        pltpu.make_async_copy(own_ref.at[:, :256], mine_ref, sems.at[2]),
    ]
    for half in range(2):
        rows = slice(half * BLOCK, (half + 1) * BLOCK)
        for number, (ref, place) in enumerate(((own_ref, core), (other_ref, 1 - core))):
            to = chunk_ref.at[pl.ds(pl.multiple_of(256 * half + BLOCK * place, BLOCK), BLOCK)]
            copies.append(
                pltpu.make_async_copy(ref.at[rows, :256], to, sems.at[3 + 2 * half + number])
            )
    for copy in copies:
        copy.start()
    for copy in copies:
        copy.wait()


def gather_pair(frame, own, other):
    rows, cols = own.shape
    vmem = pl.BlockSpec(memory_space=pltpu.VMEM)
    return pl.pallas_call(
        gather_pair_body,
        out_shape=[
            jax.ShapeDtypeStruct((2 * rows, 256), own.dtype),
            jax.ShapeDtypeStruct((2 * rows, cols - 256), own.dtype),
            jax.ShapeDtypeStruct((rows, 256), own.dtype),
        ],
        in_specs=[pl.BlockSpec(memory_space=pltpu.SMEM), vmem, vmem],
        out_specs=[vmem] * 3,
        scratch_shapes=[pltpu.SemaphoreType.DMA((7,))],
        compiler_params=pltpu.CompilerParams(vmem_limit_bytes=VMEM_BYTES),
    )(frame, own, other)


def half_body(which, frame_ref, chunk_ref, out_ref, sem):
    rows = out_ref.shape[0]
    part = frame_ref[0] % 2 if which is None else jnp.int32(which)
    at = pl.multiple_of(rows * part, rows)
    copy = pltpu.make_async_copy(chunk_ref.at[pl.ds(at, rows)], out_ref, sem)
    copy.start()
    copy.wait()


def half_of(frame, array, which=None):
    rows, cols = array.shape
    vmem = pl.BlockSpec(memory_space=pltpu.VMEM)
    return pl.pallas_call(
        functools.partial(half_body, which),
        out_shape=jax.ShapeDtypeStruct((rows // 2, cols), array.dtype),
        in_specs=[pl.BlockSpec(memory_space=pltpu.SMEM), vmem],
        out_specs=vmem,
        scratch_shapes=[pltpu.SemaphoreType.DMA],
        compiler_params=pltpu.CompilerParams(vmem_limit_bytes=VMEM_BYTES),
    )(frame, array)


def scale_body(gated_ref, square_ref, gain_ref, out_ref):
    eye = lax.broadcasted_iota(jnp.int32, (BLOCK, BLOCK), 0) == lax.broadcasted_iota(
        jnp.int32, (BLOCK, BLOCK), 1
    )
    for slot in range(2):
        rows = slice(slot * BLOCK, (slot + 1) * BLOCK)
        square = sum(square_ref[part, slot : slot + 1, :] for part in range(square_ref.shape[0]))
        scale = lax.rsqrt(square / (HEADS * HEAD_DIM) + EPS)
        column = jnp.sum(jnp.where(eye, scale, 0.0), axis=1, keepdims=True)
        out_ref[rows, :] = (gated_ref[rows, :] * column * gain_ref[...]).astype(jnp.bfloat16)


def scale_rows(gated, squares, gain):
    return pl.pallas_call(
        scale_body,
        out_shape=jax.ShapeDtypeStruct(gated.shape, jnp.bfloat16),
        in_specs=[pl.BlockSpec(memory_space=pltpu.VMEM)] * 3,
        out_specs=pl.BlockSpec(memory_space=pltpu.VMEM),
        compiler_params=pltpu.CompilerParams(vmem_limit_bytes=VMEM_BYTES),
    )(gated, squares, gain)


def along(hops):
    return [(2 * z, 2 * ((z + hops) % CHIPS)) for z in range(CHIPS)] + [
        (2 * z + 1, 2 * ((z - hops) % CHIPS) + 1) for z in range(CHIPS)
    ]


def send(array, hops):
    return lax.ppermute(array, "frame", along(hops))


def swap(array):
    return lax.ppermute(array, "frame", [(d, d ^ 1) for d in range(2 * CHIPS)])


def after(array, state):
    array, *state = lax.optimization_barrier((array, *state))
    return array, state


def body(queries, keys, values, block_mask, section_ids, section_gate, norm_gain):
    frame = lax.axis_index("frame")
    here = frame.reshape(1)
    own = pack(keys, values, queries)
    chunk, both, mine = gather_pair(here, own, swap(own))
    places = [frame, BLOCKS - 1 - frame, frame ^ 1, BLOCKS - 1 - (frame ^ 1)]
    meta = jnp.concatenate(
        [lax.dynamic_slice_in_dim(block_mask, place, 1, 0) for place in places]
        + [jnp.full((1, BLOCKS), frame, jnp.int32)],
        axis=0,
    )
    s2 = send(chunk, 2)
    s1 = send(chunk, 1)
    state = attend([("own", 0)], [mine], meta, both, None)
    s2, state = after(s2, state)
    s4 = send(s2, 2)
    s3 = send(s2, 1)
    state = attend([("whole", 1), ("whole", 2)], [s1, s2], meta, both, state)
    s4, state = after(s4, state)
    s6 = send(s4, 2)
    s5 = send(s4, 1)
    state = attend([("whole", 3), ("whole", 4)], [s3, s4], meta, both, state)
    s6, state = after(s6, state)
    half = half_of(here, s6)
    half, s6 = lax.optimization_barrier((half, s6))
    s8 = send(half, 2)
    s7 = send(s6, 1)
    state = attend([("whole", 5), ("whole", 6)], [s5, s6], meta, both, state)
    *state, theirs = attend(
        [("whole", 7), ("half", 8)], [s7, s8], meta, both, state, last=True
    )
    gated, squares = finish(meta, section_ids, section_gate, state, swap(theirs))
    squares = lax.all_gather(squares, "head", axis=0)
    return scale_rows(gated, squares, norm_gain.reshape(1, -1))


def solution(mesh):
    in_specs = (
        P(("stream", "frame"), "head"),
        P(("stream", "frame"), "head"),
        P(("stream", "frame"), "head"),
        P("stream", None),
        P("stream"),
        P(None, "head"),
        P("head"),
    )
    out_specs = P(("stream", "frame"), "head")
    return jax.shard_map(body, mesh=mesh, in_specs=in_specs, out_specs=out_specs, check_vma=False)
```

```python
import functools
import math

import jax
import jax.numpy as jnp
from jax import lax
from jax.experimental import pallas as pl
from jax.experimental.pallas import tpu as pltpu
from jax.sharding import PartitionSpec as P

HEADS = 24
HEAD_DIM = 128
LOCAL_HEADS = 6
BLOCK = 128
BLOCKS = 64
CHIPS = 16
EPS = 1e-06
TO_LOG2 = HEAD_DIM ** (-0.5) * math.log2(math.e)
LOW = -1e30
VMEM_BYTES = 16 * 1024 * 1024


def attend_body(pieces, slots, first, last, *refs):
    refs = list(refs)
    meta, q_ref = refs.pop(0), refs.pop(0)
    arrays = [refs.pop(0) for _ in pieces]
    if not first:
        del refs[:3]
    acc_ref, sum_ref, max_ref = refs.pop(0), refs.pop(0), refs.pop(0)
    if last:
        pack_ref, level_rows = refs

    frame = meta[4, 0]
    chip = frame // 2
    core = frame % 2
    groups = [[], []]
    for ref, (how, distance) in zip(arrays, pieces):
        source = lax.rem(chip - (1 - 2 * core) * distance + CHIPS, CHIPS)
        low = (2 * source, 2 * source + 1)
        high = (BLOCKS - 1 - 2 * source, BLOCKS - 2 - 2 * source)
        if how == "own":
            groups[0].append((ref, slice(0, 256), (frame, BLOCKS - 1 - frame)))
        elif how == "whole":
            groups[0].append((ref, slice(0, 256), low))
            groups[1].append((ref, slice(256, 512), high))
        else:
            places = tuple(jnp.where(core == 0, one, other) for one, other in zip(low, high))
            groups[0].append((ref, slice(0, 256), places))
    if first:
        acc_ref[...] = jnp.zeros_like(acc_ref)
        sum_ref[...] = jnp.zeros_like(sum_ref)
        max_ref[...] = jnp.full_like(max_ref, LOW)
    heads = [slice(head * HEAD_DIM, (head + 1) * HEAD_DIM) for head in range(LOCAL_HEADS)]

    def add(tiles, slot, lives):
        rows = pl.ds(pl.multiple_of(slot * BLOCK, BLOCK), BLOCK)
        width = 256 * len(tiles)
        keys = jnp.concatenate([ref[at, :HEAD_DIM] for ref, at, _ in tiles], axis=0)
        values = jnp.concatenate([ref[at, HEAD_DIM:] for ref, at, _ in tiles], axis=0)
        values = jnp.concatenate([values, jnp.ones((width, HEAD_DIM), jnp.bfloat16)], axis=1)
        before = [(max_ref[rows, cols], acc_ref[rows, cols], sum_ref[rows, cols]) for cols in heads]
        scores_of = [
            lax.dot_general(
                q_ref[rows, cols], keys, (((1,), (1,)), ((), ())), preferred_element_type=jnp.float32
            )
            for cols in heads
        ]
        if lives is not None:
            bias = jnp.concatenate(
                [
                    jnp.broadcast_to(jnp.where(live > 0, 0.0, LOW).astype(jnp.float32), (1, BLOCK))
                    for live in lives
                ],
                axis=1,
            )
            scores_of = [scores + bias for scores in scores_of]
        results = []
        for scores, (prior, acc, total) in zip(scores_of, before):
            now = jnp.maximum(prior, jnp.max(scores, axis=1, keepdims=True))
            top = now * TO_LOG2
            weights = jnp.exp2(scores * TO_LOG2 - jnp.concatenate([top] * (width // BLOCK), axis=1))
            shrink = jnp.exp2(prior * TO_LOG2 - top)
            added = jnp.dot(weights.astype(jnp.bfloat16), values, preferred_element_type=jnp.float32)
            results.append((now, acc * shrink + added[:, :HEAD_DIM], total * shrink + added[:, HEAD_DIM:]))
        for cols, (now, acc, total) in zip(heads, results):
            max_ref[rows, cols], acc_ref[rows, cols], sum_ref[rows, cols] = now, acc, total

    for tiles in groups:
        if not tiles:
            continue

        def per_slot(slot, carry, tiles=tiles):
            lives = [meta[slot, place] for _, _, places in tiles for place in places]
            count = sum(lives)

            @pl.when(count == len(lives))
            def _():
                add(tiles, slot, None)

            @pl.when(jnp.logical_and(count > 0, count < len(lives)))
            def _():
                add(tiles, slot, lives)

            return carry

        lax.fori_loop(slots[0], slots[1], per_slot, 0)

    if last:
        eye = diagonal()
        for slot in range(2):
            rows = slice((2 + slot) * BLOCK, (3 + slot) * BLOCK)
            to = slice(slot * BLOCK, (slot + 1) * BLOCK)
            for head in range(LOCAL_HEADS):
                cols = slice(head * HEAD_DIM, (head + 1) * HEAD_DIM)
                total = jnp.maximum(sum_ref[rows, cols], 1e-30)
                pack_ref[to, cols] = (acc_ref[rows, cols] / total).astype(jnp.bfloat16)
                level = max_ref[rows, cols] * TO_LOG2 + jnp.log2(total)
                level = jnp.sum(jnp.where(eye, level, 0.0), axis=0, keepdims=True)
                parts = []
                for _ in range(3):
                    part = level.astype(jnp.bfloat16).astype(jnp.float32)
                    level = level - part
                    parts.append(part)
                parts.append(jnp.zeros((5, HEAD_DIM), jnp.float32))
                level_rows[8 * slot : 8 * slot + 8, cols] = jnp.concatenate(parts, axis=0)
        pack_ref[2 * BLOCK :, :] = level_rows[...].astype(jnp.bfloat16)


def diagonal():
    return lax.broadcasted_iota(jnp.int32, (BLOCK, BLOCK), 0) == lax.broadcasted_iota(
        jnp.int32, (BLOCK, BLOCK), 1
    )


def attend(pieces, arrays, meta, queries, state, last=False, slots=(0, 4)):
    first = state is None
    tiles = sum(array.shape[0] // 256 for array in arrays)
    rows, cols = queries.shape
    vmem, smem = pl.BlockSpec(memory_space=pltpu.VMEM), pl.BlockSpec(memory_space=pltpu.SMEM)
    operands = [meta, queries, *arrays]
    in_specs = [smem] + [vmem] * (1 + len(arrays))
    aliases = {}
    if not first:
        aliases = {len(operands) + number: number for number in range(3)}
        operands += list(state)
        in_specs += [vmem] * 3
    out_shape = [jax.ShapeDtypeStruct((rows, cols), jnp.float32)] * 3
    scratch = []
    if last:
        out_shape.append(jax.ShapeDtypeStruct((rows // 2 + 16, cols), jnp.bfloat16))
        scratch.append(pltpu.VMEM((16, cols), jnp.float32))
    pairs = tiles * (slots[1] - slots[0]) * LOCAL_HEADS
    return pl.pallas_call(
        functools.partial(attend_body, pieces, slots, first, last),
        out_shape=out_shape,
        in_specs=in_specs,
        out_specs=[vmem] * len(out_shape),
        scratch_shapes=scratch,
        input_output_aliases=aliases,
        compiler_params=pltpu.CompilerParams(vmem_limit_bytes=VMEM_BYTES),
        cost_estimate=pl.CostEstimate(
            flops=pairs * 4 * BLOCK * 256 * HEAD_DIM,
            bytes_accessed=8 * rows * cols * 4,
            transcendentals=pairs * BLOCK * 256,
        ),
    )(*operands)


def finish_body(frame_ref, ids_ref, gate_ref, acc_ref, sum_ref, max_ref, theirs, gated_ref, square_ref):
    frame = frame_ref[4, 0]
    places = (frame, BLOCKS - 1 - frame)
    eye = diagonal()
    for slot in range(2):
        rows = slice(slot * BLOCK, (slot + 1) * BLOCK)
        gate_row = gate_ref[pl.ds(ids_ref[places[slot]], 1), :]
        parts = theirs[2 * BLOCK :, :].astype(jnp.float32)[8 * slot : 8 * slot + 3]
        levels = parts[0:1] + parts[1:2] + parts[2:3]
        total = jnp.zeros((BLOCK, HEAD_DIM), jnp.float32)
        for head in range(LOCAL_HEADS):
            cols = slice(head * HEAD_DIM, (head + 1) * HEAD_DIM)
            level = jnp.sum(jnp.where(eye, levels[:, cols], 0.0), axis=1, keepdims=True)
            prior = max_ref[rows, cols] * TO_LOG2
            top = jnp.maximum(prior, level)
            mine, yours = jnp.exp2(prior - top), jnp.exp2(level - top)
            joined = acc_ref[rows, cols] * mine + theirs[rows, cols].astype(jnp.float32) * yours
            gated = joined / (sum_ref[rows, cols] * mine + yours) * gate_row[:, cols]
            gated_ref[rows, cols] = gated
            total = total + gated * gated
        row_total = jnp.sum(total, axis=1, keepdims=True)
        square_ref[slot : slot + 1, :] = jnp.sum(jnp.where(eye, row_total, 0.0), axis=0, keepdims=True)


def finish(meta, section_ids, section_gate, state, theirs):
    cols = theirs.shape[1]
    vmem, smem = pl.BlockSpec(memory_space=pltpu.VMEM), pl.BlockSpec(memory_space=pltpu.SMEM)
    return pl.pallas_call(
        finish_body,
        out_shape=[
            jax.ShapeDtypeStruct((2 * BLOCK, cols), jnp.float32),
            jax.ShapeDtypeStruct((2, BLOCK), jnp.float32),
        ],
        in_specs=[smem, smem] + [vmem] * 5,
        out_specs=[vmem, vmem],
        compiler_params=pltpu.CompilerParams(vmem_limit_bytes=VMEM_BYTES),
    )(meta, section_ids, section_gate, *state, theirs)


def pack_body(keys_ref, values_ref, queries_ref, out_ref, sems):
    copies = []
    at = 0
    for number, ref in enumerate((keys_ref, values_ref, queries_ref)):
        to = out_ref.at[:, at : at + ref.shape[1]]
        copies.append(pltpu.make_async_copy(ref, to, sems.at[number]))
        at += ref.shape[1]
    for copy in copies:
        copy.start()
    for copy in copies:
        copy.wait()


def pack(keys, values, queries):
    anywhere = pl.BlockSpec(memory_space=pltpu.HBM)
    cols = keys.shape[1] + values.shape[1] + queries.shape[1]
    return pl.pallas_call(
        pack_body,
        out_shape=jax.ShapeDtypeStruct((keys.shape[0], cols), keys.dtype),
        in_specs=[anywhere] * 3,
        out_specs=pl.BlockSpec(memory_space=pltpu.VMEM),
        scratch_shapes=[pltpu.SemaphoreType.DMA((3,))],
        compiler_params=pltpu.CompilerParams(vmem_limit_bytes=VMEM_BYTES),
    )(*(pltpu.with_memory_space_constraint(array, pltpu.HBM) for array in (keys, values, queries)))


def gather_pair_body(frame_ref, own_ref, other_ref, chunk_ref, both_ref, mine_ref, sems):
    core = frame_ref[0] % 2
    copies = [
        pltpu.make_async_copy(own_ref.at[:, 256:], both_ref.at[0:256], sems.at[0]),
        pltpu.make_async_copy(other_ref.at[:, 256:], both_ref.at[256:512], sems.at[1]),
        pltpu.make_async_copy(own_ref.at[:, :256], mine_ref, sems.at[2]),
    ]
    for half in range(2):
        rows = slice(half * BLOCK, (half + 1) * BLOCK)
        for number, (ref, place) in enumerate(((own_ref, core), (other_ref, 1 - core))):
            to = chunk_ref.at[pl.ds(pl.multiple_of(256 * half + BLOCK * place, BLOCK), BLOCK)]
            copies.append(
                pltpu.make_async_copy(ref.at[rows, :256], to, sems.at[3 + 2 * half + number])
            )
    for copy in copies:
        copy.start()
    for copy in copies:
        copy.wait()


def gather_pair(frame, own, other):
    rows, cols = own.shape
    vmem = pl.BlockSpec(memory_space=pltpu.VMEM)
    return pl.pallas_call(
        gather_pair_body,
        out_shape=[
            jax.ShapeDtypeStruct((2 * rows, 256), own.dtype),
            jax.ShapeDtypeStruct((2 * rows, cols - 256), own.dtype),
            jax.ShapeDtypeStruct((rows, 256), own.dtype),
        ],
        in_specs=[pl.BlockSpec(memory_space=pltpu.SMEM), vmem, vmem],
        out_specs=[vmem] * 3,
        scratch_shapes=[pltpu.SemaphoreType.DMA((7,))],
        compiler_params=pltpu.CompilerParams(vmem_limit_bytes=VMEM_BYTES),
    )(frame, own, other)


def half_body(which, frame_ref, chunk_ref, out_ref, sem):
    rows = out_ref.shape[0]
    part = frame_ref[0] % 2 if which is None else jnp.int32(which)
    at = pl.multiple_of(rows * part, rows)
    copy = pltpu.make_async_copy(chunk_ref.at[pl.ds(at, rows)], out_ref, sem)
    copy.start()
    copy.wait()


def half_of(frame, array, which=None):
    rows, cols = array.shape
    vmem = pl.BlockSpec(memory_space=pltpu.VMEM)
    return pl.pallas_call(
        functools.partial(half_body, which),
        out_shape=jax.ShapeDtypeStruct((rows // 2, cols), array.dtype),
        in_specs=[pl.BlockSpec(memory_space=pltpu.SMEM), vmem],
        out_specs=vmem,
        scratch_shapes=[pltpu.SemaphoreType.DMA],
        compiler_params=pltpu.CompilerParams(vmem_limit_bytes=VMEM_BYTES),
    )(frame, array)


def scale_body(gated_ref, square_ref, gain_ref, out_ref):
    eye = lax.broadcasted_iota(jnp.int32, (BLOCK, BLOCK), 0) == lax.broadcasted_iota(
        jnp.int32, (BLOCK, BLOCK), 1
    )
    for slot in range(2):
        rows = slice(slot * BLOCK, (slot + 1) * BLOCK)
        square = sum(square_ref[part, slot : slot + 1, :] for part in range(square_ref.shape[0]))
        scale = lax.rsqrt(square / (HEADS * HEAD_DIM) + EPS)
        column = jnp.sum(jnp.where(eye, scale, 0.0), axis=1, keepdims=True)
        out_ref[rows, :] = (gated_ref[rows, :] * column * gain_ref[...]).astype(jnp.bfloat16)


def scale_rows(gated, squares, gain):
    return pl.pallas_call(
        scale_body,
        out_shape=jax.ShapeDtypeStruct(gated.shape, jnp.bfloat16),
        in_specs=[pl.BlockSpec(memory_space=pltpu.VMEM)] * 3,
        out_specs=pl.BlockSpec(memory_space=pltpu.VMEM),
        compiler_params=pltpu.CompilerParams(vmem_limit_bytes=VMEM_BYTES),
    )(gated, squares, gain)


def along(hops):
    return [(2 * z, 2 * ((z + hops) % CHIPS)) for z in range(CHIPS)] + [
        (2 * z + 1, 2 * ((z - hops) % CHIPS) + 1) for z in range(CHIPS)
    ]


def send(array, hops):
    return lax.ppermute(array, "frame", along(hops))


def swap(array):
    return lax.ppermute(array, "frame", [(d, d ^ 1) for d in range(2 * CHIPS)])


def after(array, state):
    array, *state = lax.optimization_barrier((array, *state))
    return array, state


def body(queries, keys, values, block_mask, section_ids, section_gate, norm_gain):
    frame = lax.axis_index("frame")
    here = frame.reshape(1)
    own = pack(keys, values, queries)
    chunk, both, mine = gather_pair(here, own, swap(own))
    places = [frame, BLOCKS - 1 - frame, frame ^ 1, BLOCKS - 1 - (frame ^ 1)]
    meta = jnp.concatenate(
        [lax.dynamic_slice_in_dim(block_mask, place, 1, 0) for place in places]
        + [jnp.full((1, BLOCKS), frame, jnp.int32)],
        axis=0,
    )
    s2 = send(chunk, 2)
    s1 = send(chunk, 1)
    state = attend([("own", 0)], [mine], meta, both, None)
    s2, state = after(s2, state)
    s4 = send(s2, 2)
    s3 = send(s2, 1)
    state = attend([("whole", 1), ("whole", 2)], [s1, s2], meta, both, state)
    s4, state = after(s4, state)
    s6 = send(s4, 2)
    s5 = send(s4, 1)
    state = attend([("whole", 3), ("whole", 4)], [s3, s4], meta, both, state)
    s6, state = after(s6, state)
    half = half_of(here, s6)
    half, s6 = lax.optimization_barrier((half, s6))
    s8 = send(half, 2)
    s7 = send(s6, 1)
    state = attend([("whole", 5), ("whole", 6)], [s5, s6], meta, both, state)
    final = [("whole", 7), ("half", 8)]
    *state, theirs = attend(final, [s7, s8], meta, both, state, last=True, slots=(2, 4))
    theirs = swap(theirs)
    state = attend(final, [s7, s8], meta, both, state, slots=(0, 2))
    gated, squares = finish(meta, section_ids, section_gate, state, theirs)
    squares = lax.all_gather(squares, "head", axis=0)
    return scale_rows(gated, squares, norm_gain.reshape(1, -1))


def solution(mesh):
    in_specs = (
        P(("stream", "frame"), "head"),
        P(("stream", "frame"), "head"),
        P(("stream", "frame"), "head"),
        P("stream", None),
        P("stream"),
        P(None, "head"),
        P("head"),
    )
    out_specs = P(("stream", "frame"), "head")
    return jax.shard_map(body, mesh=mesh, in_specs=in_specs, out_specs=out_specs, check_vma=False)
```
